32 devices in a mesh: surf: 4 (over y, core), line: 8 (over z, x).
Axes of the slice: x: 2, y: 2, z: 4, core: 2. Of those that a mesh axis runs over, the one named last changes fastest.
Arguments:
- inv_block: bfloat16 [16, 16, 320, 320], P('surf', 'line'), as said below
- couple_block: bfloat16 [16, 16, 320, 320], P('surf', 'line')
- face_block: bfloat16 [16, 16, 320, 320], P('surf', 'line'), may hold values from -0.03125 to 0.03125
- rhs: bfloat16 [16, 16, 320, 64], P('surf', 'line'), may hold values from -0.59765625 to 0.59765625
- adjoint_prev: bfloat16 [16, 16, 320, 64], P('surf', 'line'), may hold values from -6 to 6
- nb_line: int32 [16], P('surf'), may hold values from 0 to 15
- send_list: int32 [4, 4, 4], P('surf'), may hold values from 0 to 7, as said below
- send_count: int32 [4, 4], P('surf'), may hold values from 0 to 4
- recv_list: int32 [4, 4, 4], P('surf'), may hold values from 0 to 7, as said below
Outputs:
- adjoint: bfloat16 [16, 16, 320, 64], P('surf', 'line')
The draws below stay inside these ranges and needn't reach their ends.
Inputs may be any that keep to these rules, and one draw needn't show every extreme that they name: `send_list`: for every sender s the blocks it sends to all peers are 8 distinct positions; every receiver gets 4 * 2 blocks in all at distinct positions. Each device sends 4 blocks to one peer and none to another. Slots at or past the count are unused. `recv_list`: entries of slots at or past the sender's count are unused. `inv_block`: every block is the identity plus a small perturbation, its rows scaled by per-row factors below one.
All inputs are finite; a program needn't handle non-finite values.
Results may differ from the reference program's by a relative error of at most 0.0013.
Values may be sent and summed in bfloat16 or wider, within the bound.
A program may use at most 320 MiB of HBM per device.

```python
import math
import jax
import jax.numpy as jnp
from jax import lax

CELL_UNKNOWNS = 320
K = 64
LS = 4
E = 2
STRAND_TOTAL = 16
CELLS_PER_STRAND = 16
CAP = 4
N_SURF = 4
N_LINE = 8


def draw_inv_block(key, part):
    slow_share = 0.5
    is_slow = jax.random.uniform(jax.random.fold_in(key, 7), (CELL_UNKNOWNS,)) < slow_share
    inflow_frequency = jnp.where(is_slow, math.exp(-1.0 / CELLS_PER_STRAND), math.exp(-1.0 / 40.0))
    spike_occurrences = jnp.where(jax.random.uniform(jax.random.fold_in(key, 11), (STRAND_TOTAL, CELLS_PER_STRAND, 1, 1)) < 2.0 / CELLS_PER_STRAND, 0.65, 1.0)
    stochastic_perturbation = jax.random.normal(jax.random.fold_in(key, 3), (STRAND_TOTAL, CELLS_PER_STRAND, CELL_UNKNOWNS, CELL_UNKNOWNS)) * (0.2 / math.sqrt(CELL_UNKNOWNS))
    linearized_operator = (jnp.eye(CELL_UNKNOWNS, dtype=jnp.float32) + stochastic_perturbation) * inflow_frequency[None, None, :, None] * spike_occurrences * math.exp(-0.02)
    return linearized_operator.astype(jnp.bfloat16)


def draw_couple_block(key, part):
    stochastic_perturbation = jax.random.normal(jax.random.fold_in(key, 5), (STRAND_TOTAL, CELLS_PER_STRAND, CELL_UNKNOWNS, CELL_UNKNOWNS)) * (0.2 / math.sqrt(CELL_UNKNOWNS))
    return (-(jnp.eye(CELL_UNKNOWNS, dtype=jnp.float32) + stochastic_perturbation)).astype(jnp.bfloat16)


def migration_plan(key):
    per_device = LS * E
    share = per_device // N_SURF
    ranks = jnp.arange(N_SURF, dtype=jnp.int32)
    empty_offset = (2 + jax.random.randint(jax.random.fold_in(key, 101), (), 0, N_SURF - 1)) % N_SURF
    double_offset = (empty_offset + 1 + jax.random.randint(jax.random.fold_in(key, 104), (), 0, N_SURF - 1)) % N_SURF
    weights = jnp.where(ranks == double_offset, 2 * share, jnp.where(ranks == empty_offset, 0, share)).astype(jnp.int32)
    senders = ranks[:, None]
    receivers = ranks[None, :]
    counts = weights[(receivers - senders) % N_SURF]
    counts_back = counts.T
    send_start = jnp.cumsum(counts, axis=1) - counts
    recv_start = jnp.cumsum(counts_back, axis=1) - counts_back
    send_perm = jax.vmap(lambda one_key: jax.random.permutation(one_key, per_device))(jax.random.split(jax.random.fold_in(key, 102), N_SURF))
    recv_perm = jax.vmap(lambda one_key: jax.random.permutation(one_key, per_device))(jax.random.split(jax.random.fold_in(key, 103), N_SURF))
    slot_ids = jnp.arange(CAP, dtype=jnp.int32)[None, None, :]
    send_pos = jnp.clip(send_start[:, :, None] + slot_ids, 0, per_device - 1).reshape(N_SURF, -1)
    recv_pos = jnp.clip(recv_start[:, :, None] + slot_ids, 0, per_device - 1).reshape(N_SURF, -1)
    send_list = jnp.take_along_axis(send_perm, send_pos, axis=1).reshape(N_SURF, N_SURF, CAP)
    recv_list = jnp.take_along_axis(recv_perm, recv_pos, axis=1).reshape(N_SURF, N_SURF, CAP)
    send_list = jnp.where(slot_ids < counts[:, :, None], send_list, 0)
    recv_list = jnp.where(slot_ids < counts_back[:, :, None], recv_list, 0)
    return (counts.astype(jnp.int32), send_list.astype(jnp.int32), recv_list.astype(jnp.int32))


def draw_send_list(key, part):
    return migration_plan(key)[1]


def draw_send_count(key, part):
    return migration_plan(key)[0]


def draw_recv_list(key, part):
    return migration_plan(key)[2]


def touch_ends(entries, stream_key, low, high):
    extent = entries.shape
    index_at = [jax.random.randint(jax.random.fold_in(stream_key, axis), (), 0, extent[axis]) for axis in range(len(extent))]
    entries = entries.at[tuple(index_at)].set(low)
    longest = extent.index(max(extent))
    index_at[longest] = (index_at[longest] + 1) % extent[longest]
    return entries.at[tuple(index_at)].set(high)


def levels(own_key, shape, pieces, low, high):
    loudness = 1.0
    for position, blocks in pieces:
        heights = jax.random.uniform(jax.random.fold_in(jax.random.fold_in(own_key, 6), position), (blocks,), jnp.float32, low / len(pieces), high / len(pieces))
        loudness = loudness * jnp.repeat(jnp.exp(heights), shape[position] // blocks).reshape((-1,) + (1,) * (len(shape) - 1 - position))
    return loudness


def gaussian(stream_key, extent, scale, most, pieces=(), kind=jnp.bfloat16):
    gain = levels(stream_key, extent, pieces, -0.22, 0.18) if pieces else 1.0
    drawn = jax.random.normal(stream_key, extent, jnp.float32) * scale * gain
    return jnp.minimum(jnp.maximum(drawn, -most), most).astype(kind)


def setup_inputs(seed: int = 0) -> dict:
    streams_of = jax.random.split(jax.random.key(seed), 10)
    return {
        "inv_block": draw_inv_block(jax.random.fold_in(streams_of[9], 71), 0),
        "couple_block": draw_couple_block(jax.random.fold_in(streams_of[9], 71), 0),
        "face_block": gaussian(streams_of[2], (STRAND_TOTAL, CELLS_PER_STRAND, CELL_UNKNOWNS, CELL_UNKNOWNS), (100 * CELL_UNKNOWNS) ** -0.5, 0.03125, ((0, 4), (1, 8))),
        "rhs": gaussian(streams_of[3], (STRAND_TOTAL, CELLS_PER_STRAND, CELL_UNKNOWNS, K), 0.1, 0.59765625, ((0, 4), (1, 8))),
        "adjoint_prev": gaussian(streams_of[4], (STRAND_TOTAL, CELLS_PER_STRAND, CELL_UNKNOWNS, K), 1.0, 6.0, ((0, 4), (1, 8))),
        "nb_line": touch_ends(jax.random.randint(streams_of[5], (STRAND_TOTAL,), 0, STRAND_TOTAL), jax.random.fold_in(streams_of[5], 1), 0, STRAND_TOTAL - 1).astype(jnp.int32),
        "send_list": draw_send_list(jax.random.fold_in(streams_of[9], 71), 0),
        "send_count": draw_send_count(jax.random.fold_in(streams_of[9], 71), 0),
        "recv_list": draw_recv_list(jax.random.fold_in(streams_of[9], 71), 0),
    }


HIGH = lax.Precision.HIGHEST


def migrate(blocks, send_list, send_count, recv_list):
    tail = blocks.shape[2:]
    per_device = LS * E
    grouped = blocks.reshape((N_SURF, LS, N_LINE, E) + tail)
    grouped = jnp.moveaxis(grouped, 2, 0).reshape((N_LINE, N_SURF * per_device) + tail)
    senders = jnp.arange(N_SURF, dtype=jnp.int32)[:, None, None]
    receivers = jnp.arange(N_SURF, dtype=jnp.int32)[None, :, None]
    slot_ids = jnp.arange(CAP, dtype=jnp.int32)[None, None, :]
    sources = senders * per_device + send_list
    targets = receivers * per_device + jnp.transpose(recv_list, (1, 0, 2))
    is_valid = slot_ids < send_count[:, :, None]
    targets = jnp.where(is_valid, targets, N_SURF * per_device).astype(jnp.int32)
    placed = jnp.zeros_like(grouped).at[:, targets.reshape(-1)].set(grouped[:, sources.reshape(-1)], mode="drop")
    placed = placed.reshape((N_LINE, N_SURF, LS, E) + tail)
    return jnp.moveaxis(placed, 0, 2).reshape(blocks.shape)


def reference(inv_block, couple_block, face_block, rhs, adjoint_prev, nb_line, send_list, send_count, recv_list):
    inv_moved = migrate(inv_block, send_list, send_count, recv_list)
    couple_moved = migrate(couple_block, send_list, send_count, recv_list)
    face_moved = migrate(face_block, send_list, send_count, recv_list)
    rhs_moved = migrate(rhs, send_list, send_count, recv_list)
    neighbors = adjoint_prev[nb_line].astype(jnp.float32)
    neighbor_term = jnp.einsum("lebc,lecd->lebd", face_moved.astype(jnp.float32), neighbors, precision=HIGH)
    forcing = rhs_moved.astype(jnp.float32) - neighbor_term

    def step_back(carry, items):
        inv_elem, couple_elem, forcing_elem = items
        drive = forcing_elem - jnp.einsum("lbc,lcd->lbd", couple_elem.astype(jnp.float32), carry, precision=HIGH)
        swept = jnp.einsum("lbc,lcd->lbd", inv_elem.astype(jnp.float32), drive, precision=HIGH)
        return swept, swept

    outer = jnp.zeros((STRAND_TOTAL, CELL_UNKNOWNS, K), jnp.float32)
    items = (jnp.moveaxis(inv_moved, 1, 0), jnp.moveaxis(couple_moved, 1, 0), jnp.moveaxis(forcing, 1, 0))
    _, sweep = lax.scan(step_back, outer, items, reverse=True)
    return jnp.moveaxis(sweep, 0, 1).astype(jnp.bfloat16)
```

```python
import functools

import jax
import jax.numpy as jnp
from jax import lax
from jax.experimental import pallas as pl
from jax.experimental.pallas import tpu as pltpu
from jax.sharding import PartitionSpec as P

MESH = pl.DeviceIdType.MESH
F32 = jnp.float32
BF16 = jnp.bfloat16


def dot(a, b):
    return jnp.dot(a, b, preferred_element_type=F32)


def split(value):
    high = value.astype(BF16)
    return high, (value - high.astype(F32)).astype(BF16)


def line_kernel(
    n, lines, elems, slot_ref, blocks_ref, forcing_ref, out_ref,
    first_hi, first_lo, map_hi, map_lo, first_shift, shift, going, coming, send_sem, recv_sem,
):
    me = lax.axis_index("line")
    size = blocks_ref.shape[1]
    cols = forcing_ref.shape[2] // 2
    inner, outer = jnp.maximum(me - 1, 0), jnp.minimum(me + 1, n - 1)
    barrier = pltpu.get_barrier_semaphore()

    @pl.when(me < n - 1)
    def _():
        pl.semaphore_signal(barrier, inc=1, device_id={"line": outer}, device_id_type=MESH)

    @pl.when(me > 0)
    def _():
        pl.semaphore_wait(barrier, 1)

    def segment(l, _):
        outside, inside = slot_ref[l * elems + 1], slot_ref[l * elems]
        pair = blocks_ref[outside]
        inv, couple = pair[:, :size], pair[:, size:]
        force = forcing_ref[outside]
        a_hi, a_lo = split(-dot(inv, couple))
        moved = dot(inv, force)
        moved = moved[:, :cols] + moved[:, cols:]
        first_hi[l] = a_hi
        first_lo[l] = a_lo
        first_shift[l] = moved
        f_hi, f_lo = split(moved)
        pair = blocks_ref[inside]
        inv, couple = pair[:, :size], pair[:, size:]
        force = forcing_ref[inside].astype(F32)
        force = force[:, :cols] + force[:, cols:]
        d_hi, d_lo = split(-(dot(couple, a_hi) + dot(couple, a_lo)))
        g_hi, g_lo = split(force - (dot(couple, f_hi) + dot(couple, f_lo)))
        m_hi, m_lo = split(dot(inv, d_hi) + dot(inv, d_lo))
        map_hi[l] = m_hi
        map_lo[l] = m_lo
        shift[l] = dot(inv, g_hi) + dot(inv, g_lo)
        return 0

    lax.fori_loop(0, lines, segment, 0)

    def copy(l):
        return pltpu.make_async_remote_copy(
            src_ref=going.at[l], dst_ref=coming.at[l], send_sem=send_sem.at[l],
            recv_sem=recv_sem.at[l], device_id={"line": inner}, device_id_type=MESH,
        )

    @pl.when(me == n - 1)
    def _():
        coming[...] = jnp.zeros_like(coming)

    def applied(hi, lo, value):
        both = dot(hi, value)
        return both[:, :cols] + (both[:, cols:] + dot(lo, value[:, :cols]))

    for l in range(lines):
        @pl.when(me < n - 1)
        def _():
            copy(l).wait_recv()

        last = shift[l] + applied(map_hi[l], map_lo[l], coming[l])
        hi, lo = split(last)
        going[l] = jnp.concatenate([hi, lo], axis=-1)

        @pl.when(me > 0)
        def _():
            copy(l).start()

        out_ref[l, 0] = hi

    for l in range(lines):
        value = first_shift[l] + applied(first_hi[l], first_lo[l], coming[l])
        out_ref[l, 1] = value.astype(BF16)

    for l in range(lines):
        @pl.when(me > 0)
        def _():
            copy(l).wait_send()


def swept(n, lines, elems, slots, blocks, forcing):
    size, cols = blocks.shape[1], forcing.shape[2] // 2
    vmem = pl.BlockSpec(memory_space=pltpu.VMEM)
    square = pltpu.VMEM((lines, size, size), BF16)
    return pl.pallas_call(
        functools.partial(line_kernel, n, lines, elems),
        out_shape=jax.ShapeDtypeStruct((lines, elems, size, cols), BF16),
        in_specs=[pl.BlockSpec(memory_space=pltpu.SMEM), vmem, vmem],
        out_specs=vmem,
        scratch_shapes=[
            square, square, square, square,
            pltpu.VMEM((lines, size, cols), F32),
            pltpu.VMEM((lines, size, cols), F32),
            pltpu.VMEM((lines, size, 2 * cols), BF16),
            pltpu.VMEM((lines, size, 2 * cols), BF16),
            pltpu.SemaphoreType.DMA((lines,)),
            pltpu.SemaphoreType.DMA((lines,)),
        ],
        compiler_params=pltpu.CompilerParams(
            collective_id=0, has_side_effects=True, vmem_limit_bytes=48 << 20
        ),
    )(slots, blocks, forcing)


def pack_kernel(pick_ref, inv_ref, couple_ref, out_ref):
    size = inv_ref.shape[2]
    out_ref[0, :, :size] = inv_ref[0, 0]
    out_ref[0, :, size:] = couple_ref[0, 0]


def packed(picks, inv_block, couple_block):
    _, elems, size, _ = inv_block.shape
    count = picks.shape[0]
    block = pl.BlockSpec(
        (1, 1, size, size), lambda s, pick: (pick[s] // elems, pick[s] % elems, 0, 0)
    )
    return pl.pallas_call(
        pack_kernel,
        out_shape=jax.ShapeDtypeStruct((count, size, 2 * size), BF16),
        grid_spec=pltpu.PrefetchScalarGridSpec(
            num_scalar_prefetch=1,
            grid=(count,),
            in_specs=[block, block],
            out_specs=pl.BlockSpec((1, size, 2 * size), lambda s, pick: (s, 0, 0)),
        ),
        cost_estimate=pl.CostEstimate(
            flops=0, bytes_accessed=8 * count * size * size, transcendentals=0
        ),
    )(picks, inv_block, couple_block)


def force_kernel(elems, pick_ref, line_ref, elem_ref, face_ref, rhs_ref, adjoint_ref, out_ref):
    cols = rhs_ref.shape[3]
    terms = dot(face_ref[0, 0], adjoint_ref[0])
    elem = elem_ref[pl.program_id(0)]
    term = terms[:, :cols]
    for e in range(1, elems):
        term = jnp.where(elem == e, terms[:, e * cols : (e + 1) * cols], term)
    hi, lo = split(rhs_ref[0, 0].astype(F32) - term)
    out_ref[0] = jnp.concatenate([hi, lo], axis=-1)


def forced(picks, lines, elem, face_block, rhs, adjoints):
    _, elems, size, _ = face_block.shape
    cols = rhs.shape[3]
    count = picks.shape[0]

    def stored_at(s, pick, line, elem):
        return (pick[s] // elems, pick[s] % elems, 0, 0)

    return pl.pallas_call(
        functools.partial(force_kernel, elems),
        out_shape=jax.ShapeDtypeStruct((count, size, 2 * cols), BF16),
        grid_spec=pltpu.PrefetchScalarGridSpec(
            num_scalar_prefetch=3,
            grid=(count,),
            in_specs=[
                pl.BlockSpec((1, 1, size, size), stored_at),
                pl.BlockSpec((1, 1, size, cols), stored_at),
                pl.BlockSpec((1, size, elems * cols), lambda s, pick, line, elem: (line[s], 0, 0)),
            ],
            out_specs=pl.BlockSpec((1, size, 2 * cols), lambda s, pick, line, elem: (s, 0, 0)),
        ),
        cost_estimate=pl.CostEstimate(
            flops=4 * count * size * size * cols, bytes_accessed=2 * count * size * size,
            transcendentals=0,
        ),
    )(picks, lines, elem, face_block, rhs, adjoints)


def per_device(n_surf, n_line, inv_block, couple_block, face_block, rhs, adjoint_prev,
               nb_line, send_list, send_count, recv_list):
    lines, elems, size, _ = inv_block.shape
    cols = rhs.shape[3]
    stored = lines * elems
    cap = send_list.shape[2]
    total = n_surf * cap
    me = lax.axis_index("surf")
    ids = jnp.arange(cap, dtype=jnp.int32)[None, :]
    ranks = jnp.arange(n_surf, dtype=jnp.int32)

    leaves = ids < send_count[0][:, None]
    picks = jnp.where(leaves, send_list[0], 0).reshape(-1)
    got_blocks = lax.all_to_all(
        packed(picks, inv_block, couple_block).reshape(n_surf, cap, size, 2 * size),
        "surf", split_axis=0, concat_axis=0, tiled=True,
    )

    table = jnp.concatenate([recv_list[0].reshape(-1), nb_line, send_count[0]])
    tables = lax.all_gather(table, "surf", axis=0, tiled=False)
    places = tables[:, : n_surf * cap].reshape(n_surf, n_surf, cap)
    nb_all = tables[:, n_surf * cap : n_surf * cap + lines].reshape(-1)
    counts = tables[:, n_surf * cap + lines :]

    mine = jnp.sum(jnp.where((ranks == me)[None, :, None], places, 0), axis=1)
    goal = jnp.where(leaves, mine + ranks[:, None] * stored, 0).reshape(-1)
    goal_line, goal_elem = goal // elems, goal % elems
    all_lines = jnp.arange(n_surf * lines, dtype=jnp.int32)
    nb = jnp.sum(jnp.where(goal_line[:, None] == all_lines[None], nb_all[None], 0), axis=1)

    lanes = jnp.concatenate([adjoint_prev[:, e] for e in range(elems)], axis=-1)
    adjoints = lax.all_gather(lanes, "surf", axis=0, tiled=True)
    halves = forced(picks, nb, goal_elem, face_block, rhs, adjoints)
    got_forcing = lax.all_to_all(
        halves.reshape(n_surf, cap, size, 2 * cols), "surf", split_axis=0, concat_axis=0, tiled=True
    )

    to_me = jnp.sum(jnp.where((ranks == me)[None], counts, 0), axis=1)
    valid = (ids < to_me[:, None]).reshape(-1)
    positions = jnp.arange(stored, dtype=jnp.int32)
    hits = (recv_list[0].reshape(-1)[None] == positions[:, None]) & valid[None]
    slots = jnp.sum(jnp.where(hits, jnp.arange(total, dtype=jnp.int32)[None], 0), axis=1)

    return swept(
        n_line, lines, elems, slots,
        got_blocks.reshape(total, size, 2 * size),
        got_forcing.reshape(total, size, 2 * cols),
    )


def solution(mesh):
    whole = P("surf", "line", None, None)
    in_specs = (
        whole, whole, whole, whole, whole,
        P("surf"), P("surf", None, None), P("surf", None), P("surf", None, None),
    )
    body = functools.partial(per_device, mesh.shape["surf"], mesh.shape["line"])
    return jax.shard_map(
        body, mesh=mesh, in_specs=in_specs, out_specs=whole, check_vma=False
    )
```

```python
import functools

import jax
import jax.numpy as jnp
from jax import lax
from jax.experimental import pallas as pl
from jax.experimental.pallas import tpu as pltpu
from jax.sharding import PartitionSpec as P

MESH = pl.DeviceIdType.MESH
F32 = jnp.float32
BF16 = jnp.bfloat16


def dot(a, b):
    return jnp.dot(a, b, preferred_element_type=F32)


def split(value):
    high = value.astype(BF16)
    return high, (value - high.astype(F32)).astype(BF16)


def line_kernel(
    n, lines, elems, n_slabs, slot_ref, *refs
):
    blocks, forces, rest = refs[:n_slabs], refs[n_slabs : 2 * n_slabs], refs[2 * n_slabs :]
    (out_ref, first_hi, first_lo, map_hi, map_lo, first_shift, shift, going, coming,
     send_sem, recv_sem) = rest
    me = lax.axis_index("line")
    cap, size, _ = blocks[0].shape
    cols = forces[0].shape[2] // 2

    def taken(slabs, slot):
        slab, place = slot // cap, slot % cap
        value = slabs[0][place]
        for d in range(1, n_slabs):
            value = jnp.where(slab == d, slabs[d][place], value)
        return value

    inner, outer = jnp.maximum(me - 1, 0), jnp.minimum(me + 1, n - 1)
    barrier = pltpu.get_barrier_semaphore()

    @pl.when(me < n - 1)
    def _():
        pl.semaphore_signal(barrier, inc=1, device_id={"line": outer}, device_id_type=MESH)

    @pl.when(me > 0)
    def _():
        pl.semaphore_wait(barrier, 1)

    def segment(l, _):
        outside, inside = slot_ref[l * elems + 1], slot_ref[l * elems]
        pair = taken(blocks, outside)
        inv, couple = pair[:, :size], pair[:, size:]
        force = taken(forces, outside)
        a_hi, a_lo = split(-dot(inv, couple))
        moved = dot(inv, force)
        moved = moved[:, :cols] + moved[:, cols:]
        first_hi[l] = a_hi
        first_lo[l] = a_lo
        first_shift[l] = moved
        f_hi, f_lo = split(moved)
        pair = taken(blocks, inside)
        inv, couple = pair[:, :size], pair[:, size:]
        force = taken(forces, inside).astype(F32)
        force = force[:, :cols] + force[:, cols:]
        d_hi, d_lo = split(-(dot(couple, a_hi) + dot(couple, a_lo)))
        g_hi, g_lo = split(force - (dot(couple, f_hi) + dot(couple, f_lo)))
        m_hi, m_lo = split(dot(inv, d_hi) + dot(inv, d_lo))
        map_hi[l] = m_hi
        map_lo[l] = m_lo
        shift[l] = dot(inv, g_hi) + dot(inv, g_lo)
        return 0

    lax.fori_loop(0, lines, segment, 0)

    def copy(l):
        return pltpu.make_async_remote_copy(
            src_ref=going.at[l], dst_ref=coming.at[l], send_sem=send_sem.at[l],
            recv_sem=recv_sem.at[l], device_id={"line": inner}, device_id_type=MESH,
        )

    @pl.when(me == n - 1)
    def _():
        coming[...] = jnp.zeros_like(coming)

    def applied(hi, lo, value):
        both = dot(hi, value)
        return both[:, :cols] + (both[:, cols:] + dot(lo, value[:, :cols]))

    for l in range(lines):
        @pl.when(me < n - 1)
        def _():
            copy(l).wait_recv()

        last = shift[l] + applied(map_hi[l], map_lo[l], coming[l])
        hi, lo = split(last)
        going[l] = jnp.concatenate([hi, lo], axis=-1)

        @pl.when(me > 0)
        def _():
            copy(l).start()

        out_ref[l, 0] = hi

    for l in range(lines):
        value = first_shift[l] + applied(first_hi[l], first_lo[l], coming[l])
        out_ref[l, 1] = value.astype(BF16)

    for l in range(lines):
        @pl.when(me > 0)
        def _():
            copy(l).wait_send()


def swept(n, lines, elems, slots, blocks, forcing):
    size, cols = blocks[0].shape[1], forcing[0].shape[2] // 2
    vmem = pl.BlockSpec(memory_space=pltpu.VMEM)
    square = pltpu.VMEM((lines, size, size), BF16)
    return pl.pallas_call(
        functools.partial(line_kernel, n, lines, elems, len(blocks)),
        out_shape=jax.ShapeDtypeStruct((lines, elems, size, cols), BF16),
        in_specs=[pl.BlockSpec(memory_space=pltpu.SMEM)] + [vmem] * (2 * len(blocks)),
        out_specs=vmem,
        scratch_shapes=[
            square, square, square, square,
            pltpu.VMEM((lines, size, cols), F32),
            pltpu.VMEM((lines, size, cols), F32),
            pltpu.VMEM((lines, size, 2 * cols), BF16),
            pltpu.VMEM((lines, size, 2 * cols), BF16),
            pltpu.SemaphoreType.DMA((lines,)),
            pltpu.SemaphoreType.DMA((lines,)),
        ],
        compiler_params=pltpu.CompilerParams(
            collective_id=0, has_side_effects=True, vmem_limit_bytes=48 << 20
        ),
    )(slots, *blocks, *forcing)


def pack_kernel(pick_ref, inv_ref, couple_ref, out_ref):
    size = inv_ref.shape[2]
    out_ref[0, :, :size] = inv_ref[0, 0]
    out_ref[0, :, size:] = couple_ref[0, 0]


def packed(picks, inv_block, couple_block):
    _, elems, size, _ = inv_block.shape
    count = picks.shape[0]
    block = pl.BlockSpec(
        (1, 1, size, size), lambda s, pick: (pick[s] // elems, pick[s] % elems, 0, 0)
    )
    return pl.pallas_call(
        pack_kernel,
        out_shape=jax.ShapeDtypeStruct((count, size, 2 * size), BF16),
        grid_spec=pltpu.PrefetchScalarGridSpec(
            num_scalar_prefetch=1,
            grid=(count,),
            in_specs=[block, block],
            out_specs=pl.BlockSpec((1, size, 2 * size), lambda s, pick: (s, 0, 0)),
        ),
        cost_estimate=pl.CostEstimate(
            flops=0, bytes_accessed=8 * count * size * size, transcendentals=0
        ),
    )(picks, inv_block, couple_block)


def force_kernel(elems, pick_ref, line_ref, elem_ref, face_ref, rhs_ref, adjoint_ref, out_ref):
    cols = rhs_ref.shape[3]
    terms = dot(face_ref[0, 0], adjoint_ref[0])
    elem = elem_ref[pl.program_id(0)]
    term = terms[:, :cols]
    for e in range(1, elems):
        term = jnp.where(elem == e, terms[:, e * cols : (e + 1) * cols], term)
    hi, lo = split(rhs_ref[0, 0].astype(F32) - term)
    out_ref[0] = jnp.concatenate([hi, lo], axis=-1)


def forced(picks, lines, elem, face_block, rhs, adjoints):
    _, elems, size, _ = face_block.shape
    cols = rhs.shape[3]
    count = picks.shape[0]

    def stored_at(s, pick, line, elem):
        return (pick[s] // elems, pick[s] % elems, 0, 0)

    return pl.pallas_call(
        functools.partial(force_kernel, elems),
        out_shape=jax.ShapeDtypeStruct((count, size, 2 * cols), BF16),
        grid_spec=pltpu.PrefetchScalarGridSpec(
            num_scalar_prefetch=3,
            grid=(count,),
            in_specs=[
                pl.BlockSpec((1, 1, size, size), stored_at),
                pl.BlockSpec((1, 1, size, cols), stored_at),
                pl.BlockSpec((1, size, elems * cols), lambda s, pick, line, elem: (line[s], 0, 0)),
            ],
            out_specs=pl.BlockSpec((1, size, 2 * cols), lambda s, pick, line, elem: (s, 0, 0)),
        ),
        cost_estimate=pl.CostEstimate(
            flops=4 * count * size * size * cols, bytes_accessed=2 * count * size * size,
            transcendentals=0,
        ),
    )(picks, lines, elem, face_block, rhs, adjoints)


def per_device(n_surf, n_line, inv_block, couple_block, face_block, rhs, adjoint_prev,
               nb_line, send_list, send_count, recv_list):
    lines, elems, size, _ = inv_block.shape
    cols = rhs.shape[3]
    stored = lines * elems
    cap = send_list.shape[2]
    me = lax.axis_index("surf")
    ids = jnp.arange(cap, dtype=jnp.int32)[None, :]
    ranks = jnp.arange(n_surf, dtype=jnp.int32)

    onward = ranks[None] == ((me + ranks) % n_surf)[:, None]

    def by_offset(rows):
        return jnp.sum(jnp.where(onward[:, :, None], rows[None], 0), axis=1)

    def moved(value, d):
        return lax.ppermute(value, "surf", [(s, (s + d) % n_surf) for s in range(n_surf)])

    leaves = ids < by_offset(send_count[0][:, None])
    picks = jnp.where(leaves, by_offset(send_list[0]), 0)
    order = sorted(range(n_surf), key=lambda d: -min(d, n_surf - d))
    pairs = {d: packed(picks[d], inv_block, couple_block) for d in order}
    got_blocks = [moved(pairs[d], d) if d else pairs[0] for d in range(n_surf)]

    table = jnp.concatenate([recv_list[0].reshape(-1), nb_line, send_count[0]])
    tables = lax.all_gather(table, "surf", axis=0, tiled=False)
    places = tables[:, : n_surf * cap].reshape(n_surf, n_surf, cap)
    nb_all = tables[:, n_surf * cap : n_surf * cap + lines].reshape(-1)
    counts = tables[:, n_surf * cap + lines :]

    mine = jnp.sum(jnp.where((ranks == me)[None, :, None], places, 0), axis=1)
    goal = jnp.where(leaves, by_offset(mine + ranks[:, None] * stored), 0)
    goal_line, goal_elem = goal // elems, goal % elems
    all_lines = jnp.arange(n_surf * lines, dtype=jnp.int32)
    nb = jnp.sum(jnp.where(goal_line[..., None] == all_lines, nb_all, 0), axis=-1)

    lanes = jnp.concatenate([adjoint_prev[:, e] for e in range(elems)], axis=-1)
    adjoints = lax.all_gather(lanes, "surf", axis=0, tiled=True)
    later, _ = lax.optimization_barrier((picks, [pairs[d] for d in order]))
    halves = {
        d: forced(later[d], nb[d], goal_elem[d], face_block, rhs, adjoints) for d in order
    }
    got_forcing = [moved(halves[d], d) if d else halves[0] for d in range(n_surf)]

    to_me = jnp.sum(jnp.where((ranks == me)[None], counts, 0), axis=1)
    valid = (ids < to_me[:, None]).reshape(-1)
    positions = jnp.arange(stored, dtype=jnp.int32)
    hits = (recv_list[0].reshape(-1)[None] == positions[:, None]) & valid[None]
    places_here = ((me - ranks) % n_surf)[:, None] * cap + ids
    slots = jnp.sum(jnp.where(hits, places_here.reshape(-1)[None], 0), axis=1)

    return swept(n_line, lines, elems, slots, got_blocks, got_forcing)


def solution(mesh):
    whole = P("surf", "line", None, None)
    in_specs = (
        whole, whole, whole, whole, whole,
        P("surf"), P("surf", None, None), P("surf", None), P("surf", None, None),
    )
    body = functools.partial(per_device, mesh.shape["surf"], mesh.shape["line"])
    return jax.shard_map(
        body, mesh=mesh, in_specs=in_specs, out_specs=whole, check_vma=False
    )
```

```python
import functools
import itertools

import jax
import jax.numpy as jnp
from jax import lax
from jax.experimental import pallas as pl
from jax.experimental.pallas import tpu as pltpu
from jax.sharding import PartitionSpec as P

MESH = pl.DeviceIdType.MESH
F32 = jnp.float32
BF16 = jnp.bfloat16


def dot(a, b):
    return jnp.dot(a, b, preferred_element_type=F32)


def split(value):
    high = value.astype(BF16)
    return high, (value - high.astype(F32)).astype(BF16)


def line_kernel(
    n, lines, elems, n_slabs, slot_ref, *refs
):
    blocks, forces, rest = refs[:n_slabs], refs[n_slabs : 2 * n_slabs], refs[2 * n_slabs :]
    (out_ref, first_hi, first_lo, map_hi, map_lo, first_shift, shift, going, coming,
     send_sem, recv_sem) = rest
    me = lax.axis_index("line")
    cap, size, _ = blocks[0].shape
    cols = forces[0].shape[2] // 2

    def taken(slabs, slot):
        slab, place = slot // cap, slot % cap
        value = slabs[0][place]
        for d in range(1, n_slabs):
            value = jnp.where(slab == d, slabs[d][place], value)
        return value

    inner, outer = jnp.maximum(me - 1, 0), jnp.minimum(me + 1, n - 1)
    barrier = pltpu.get_barrier_semaphore()

    @pl.when(me < n - 1)
    def _():
        pl.semaphore_signal(barrier, inc=1, device_id={"line": outer}, device_id_type=MESH)

    @pl.when(me > 0)
    def _():
        pl.semaphore_wait(barrier, 1)

    def segment(l, _):
        outside, inside = slot_ref[l * elems + 1], slot_ref[l * elems]
        pair = taken(blocks, outside)
        inv, couple = pair[:, :size], pair[:, size:]
        force = taken(forces, outside)
        a_hi, a_lo = split(-dot(inv, couple))
        moved = dot(inv, force)
        moved = moved[:, :cols] + moved[:, cols:]
        first_hi[l] = a_hi
        first_lo[l] = a_lo
        first_shift[l] = moved
        f_hi, f_lo = split(moved)
        pair = taken(blocks, inside)
        inv, couple = pair[:, :size], pair[:, size:]
        force = taken(forces, inside).astype(F32)
        force = force[:, :cols] + force[:, cols:]
        d_hi, d_lo = split(-(dot(couple, a_hi) + dot(couple, a_lo)))
        g_hi, g_lo = split(force - (dot(couple, f_hi) + dot(couple, f_lo)))
        m_hi, m_lo = split(dot(inv, d_hi) + dot(inv, d_lo))
        map_hi[l] = m_hi
        map_lo[l] = m_lo
        shift[l] = dot(inv, g_hi) + dot(inv, g_lo)
        return 0

    lax.fori_loop(0, lines, segment, 0)

    def copy(l):
        return pltpu.make_async_remote_copy(
            src_ref=going.at[l], dst_ref=coming.at[l], send_sem=send_sem.at[l],
            recv_sem=recv_sem.at[l], device_id={"line": inner}, device_id_type=MESH,
        )

    @pl.when(me == n - 1)
    def _():
        coming[...] = jnp.zeros_like(coming)

    def applied(hi, lo, value):
        both = dot(hi, value)
        return both[:, :cols] + (both[:, cols:] + dot(lo, value[:, :cols]))

    for l in range(lines):
        @pl.when(me < n - 1)
        def _():
            copy(l).wait_recv()

        last = shift[l] + applied(map_hi[l], map_lo[l], coming[l])
        hi, lo = split(last)
        going[l] = jnp.concatenate([hi, lo], axis=-1)

        @pl.when(me > 0)
        def _():
            copy(l).start()

        out_ref[l, 0] = hi

    for l in range(lines):
        value = first_shift[l] + applied(first_hi[l], first_lo[l], coming[l])
        out_ref[l, 1] = value.astype(BF16)

    for l in range(lines):
        @pl.when(me > 0)
        def _():
            copy(l).wait_send()


def swept(n, lines, elems, slots, blocks, forcing):
    size, cols = blocks[0].shape[1], forcing[0].shape[2] // 2
    vmem = pl.BlockSpec(memory_space=pltpu.VMEM)
    square = pltpu.VMEM((lines, size, size), BF16)
    return pl.pallas_call(
        functools.partial(line_kernel, n, lines, elems, len(blocks)),
        out_shape=jax.ShapeDtypeStruct((lines, elems, size, cols), BF16),
        in_specs=[pl.BlockSpec(memory_space=pltpu.SMEM)] + [vmem] * (2 * len(blocks)),
        out_specs=vmem,
        scratch_shapes=[
            square, square, square, square,
            pltpu.VMEM((lines, size, cols), F32),
            pltpu.VMEM((lines, size, cols), F32),
            pltpu.VMEM((lines, size, 2 * cols), BF16),
            pltpu.VMEM((lines, size, 2 * cols), BF16),
            pltpu.SemaphoreType.DMA((lines,)),
            pltpu.SemaphoreType.DMA((lines,)),
        ],
        compiler_params=pltpu.CompilerParams(
            collective_id=0, has_side_effects=True, vmem_limit_bytes=48 << 20
        ),
    )(slots, *blocks, *forcing)


def pack_kernel(pick_ref, inv_ref, couple_ref, out_ref):
    size = inv_ref.shape[2]
    out_ref[0, :, :size] = inv_ref[0, 0]
    out_ref[0, :, size:] = couple_ref[0, 0]


def packed(picks, inv_block, couple_block):
    _, elems, size, _ = inv_block.shape
    count = picks.shape[0]
    block = pl.BlockSpec(
        (1, 1, size, size), lambda s, pick: (pick[s] // elems, pick[s] % elems, 0, 0)
    )
    return pl.pallas_call(
        pack_kernel,
        out_shape=jax.ShapeDtypeStruct((count, size, 2 * size), BF16),
        grid_spec=pltpu.PrefetchScalarGridSpec(
            num_scalar_prefetch=1,
            grid=(count,),
            in_specs=[block, block],
            out_specs=pl.BlockSpec((1, size, 2 * size), lambda s, pick: (s, 0, 0)),
        ),
        cost_estimate=pl.CostEstimate(
            flops=0, bytes_accessed=8 * count * size * size, transcendentals=0
        ),
    )(picks, inv_block, couple_block)


def force_kernel(elems, pick_ref, line_ref, elem_ref, face_ref, rhs_ref, adjoint_ref, out_ref):
    cols = rhs_ref.shape[3]
    terms = dot(face_ref[0, 0], adjoint_ref[0])
    elem = elem_ref[pl.program_id(0)]
    term = terms[:, :cols]
    for e in range(1, elems):
        term = jnp.where(elem == e, terms[:, e * cols : (e + 1) * cols], term)
    hi, lo = split(rhs_ref[0, 0].astype(F32) - term)
    out_ref[0] = jnp.concatenate([hi, lo], axis=-1)


def forced(picks, lines, elem, face_block, rhs, adjoints):
    _, elems, size, _ = face_block.shape
    cols = rhs.shape[3]
    count = picks.shape[0]

    def stored_at(s, pick, line, elem):
        return (pick[s] // elems, pick[s] % elems, 0, 0)

    return pl.pallas_call(
        functools.partial(force_kernel, elems),
        out_shape=jax.ShapeDtypeStruct((count, size, 2 * cols), BF16),
        grid_spec=pltpu.PrefetchScalarGridSpec(
            num_scalar_prefetch=3,
            grid=(count,),
            in_specs=[
                pl.BlockSpec((1, 1, size, size), stored_at),
                pl.BlockSpec((1, 1, size, cols), stored_at),
                pl.BlockSpec((1, size, elems * cols), lambda s, pick, line, elem: (line[s], 0, 0)),
            ],
            out_specs=pl.BlockSpec((1, size, 2 * cols), lambda s, pick, line, elem: (s, 0, 0)),
        ),
        cost_estimate=pl.CostEstimate(
            flops=4 * count * size * size * cols, bytes_accessed=2 * count * size * size,
            transcendentals=0,
        ),
    )(picks, lines, elem, face_block, rhs, adjoints)


def per_device(n_surf, n_line, inv_block, couple_block, face_block, rhs, adjoint_prev,
               nb_line, send_list, send_count, recv_list):
    lines, elems, size, _ = inv_block.shape
    cols = rhs.shape[3]
    stored = lines * elems
    cap = send_list.shape[2]
    me = lax.axis_index("surf")
    ids = jnp.arange(cap, dtype=jnp.int32)[None, :]
    ranks = jnp.arange(n_surf, dtype=jnp.int32)

    onward = ranks[None] == ((me + ranks) % n_surf)[:, None]

    def by_offset(rows):
        return jnp.sum(jnp.where(onward[:, :, None], rows[None], 0), axis=1)

    def moved(value, d):
        return lax.ppermute(value, "surf", [(s, (s + d) % n_surf) for s in range(n_surf)])

    leaves = ids < by_offset(send_count[0][:, None])
    picks = jnp.where(leaves, by_offset(send_list[0]), 0)
    order = sorted(range(n_surf), key=lambda d: -min(d, n_surf - d))

    table = jnp.concatenate([recv_list[0].reshape(-1), nb_line, send_count[0]])
    tables = lax.all_gather(table, "surf", axis=0, tiled=False)
    places = tables[:, : n_surf * cap].reshape(n_surf, n_surf, cap)
    nb_all = tables[:, n_surf * cap : n_surf * cap + lines].reshape(-1)
    counts = tables[:, n_surf * cap + lines :]

    mine = jnp.sum(jnp.where((ranks == me)[None, :, None], places, 0), axis=1)
    goal = jnp.where(leaves, by_offset(mine + ranks[:, None] * stored), 0)
    goal_line, goal_elem = goal // elems, goal % elems
    all_lines = jnp.arange(n_surf * lines, dtype=jnp.int32)
    nb = jnp.sum(jnp.where(goal_line[..., None] == all_lines, nb_all, 0), axis=-1)

    lanes = jnp.concatenate([adjoint_prev[:, e] for e in range(elems)], axis=-1)

    def exchanged(budgets):
        def padded(value):
            room = cap - value.shape[0]
            return jnp.pad(value, ((0, room), (0, 0), (0, 0))) if room else value

        def branch():
            used = [d for d in order if budgets[d]]
            pairs = {d: packed(picks[d, : budgets[d]], inv_block, couple_block) for d in used}
            got = [moved(pairs[d], d) if d in used and d else None for d in range(n_surf)]
            adjoints = lax.all_gather(lanes, "surf", axis=0, tiled=True)
            later, _ = lax.optimization_barrier((picks, [pairs[d] for d in used]))
            halves = {
                d: forced(
                    later[d, : budgets[d]], nb[d, : budgets[d]], goal_elem[d, : budgets[d]],
                    face_block, rhs, adjoints,
                )
                for d in used
            }
            got_forcing = [
                moved(halves[d], d) if d in used and d else None for d in range(n_surf)
            ]
            got[0], got_forcing[0] = pairs[0], halves[0]
            blank = jnp.zeros((cap, size, 2 * size), BF16)
            blank_forcing = jnp.zeros((cap, size, 2 * cols), BF16)
            return (
                tuple(blank if g is None else padded(g) for g in got),
                tuple(blank_forcing if g is None else padded(g) for g in got_forcing),
            )

        return branch

    sender = ranks[None, :]
    needed = jnp.stack([
        jnp.max(jnp.sum(jnp.where((sender + d) % n_surf == ranks[:, None], counts.T, 0), axis=0))
        for d in range(n_surf)
    ])
    plans = [(cap,) * n_surf]
    if n_surf == 4 and cap % 2 == 0:
        half = cap // 2
        plans += sorted(
            {
                (cap,) + p[1:]
                for p in itertools.permutations((0, half, half, cap))
            },
            key=lambda p: -(2 * p[2] + p[1] + p[3]),
        )
    pick = jnp.int32(0)
    for i, plan in enumerate(plans):
        pick = jnp.where(jnp.all(needed <= jnp.array(plan, jnp.int32)), i, pick)
    got_blocks, got_forcing = lax.switch(pick, [exchanged(p) for p in plans])

    to_me = jnp.sum(jnp.where((ranks == me)[None], counts, 0), axis=1)
    valid = (ids < to_me[:, None]).reshape(-1)
    positions = jnp.arange(stored, dtype=jnp.int32)
    hits = (recv_list[0].reshape(-1)[None] == positions[:, None]) & valid[None]
    places_here = ((me - ranks) % n_surf)[:, None] * cap + ids
    slots = jnp.sum(jnp.where(hits, places_here.reshape(-1)[None], 0), axis=1)

    return swept(n_line, lines, elems, slots, got_blocks, got_forcing)


def solution(mesh):
    whole = P("surf", "line", None, None)
    in_specs = (
        whole, whole, whole, whole, whole,
        P("surf"), P("surf", None, None), P("surf", None), P("surf", None, None),
    )
    body = functools.partial(per_device, mesh.shape["surf"], mesh.shape["line"])
    return jax.shard_map(
        body, mesh=mesh, in_specs=in_specs, out_specs=whole, check_vma=False
    )
```

```python
import functools

import jax
import jax.numpy as jnp
from jax import lax
from jax.experimental import pallas as pl
from jax.experimental.pallas import tpu as pltpu
from jax.sharding import PartitionSpec as P

MESH = pl.DeviceIdType.MESH
F32 = jnp.float32
BF16 = jnp.bfloat16


def dot(a, b):
    return jnp.dot(a, b, preferred_element_type=F32)


def split(value):
    high = value.astype(BF16)
    return high, (value - high.astype(F32)).astype(BF16)


def line_kernel(
    n, lines, elems, n_slabs, slot_ref, *refs
):
    blocks, forces, rest = refs[:n_slabs], refs[n_slabs : 2 * n_slabs], refs[2 * n_slabs :]
    (out_ref, first_hi, first_lo, map_hi, map_lo, first_shift, shift, going, coming,
     send_sem, recv_sem) = rest
    me = lax.axis_index("line")
    cap, size, _ = blocks[0].shape
    cols = forces[0].shape[2] // 2

    def taken(slabs, slot):
        slab, place = slot // cap, slot % cap
        value = slabs[0][place]
        for d in range(1, n_slabs):
            value = jnp.where(slab == d, slabs[d][place], value)
        return value

    inner, outer = jnp.maximum(me - 1, 0), jnp.minimum(me + 1, n - 1)
    barrier = pltpu.get_barrier_semaphore()

    @pl.when(me < n - 1)
    def _():
        pl.semaphore_signal(barrier, inc=1, device_id={"line": outer}, device_id_type=MESH)

    @pl.when(me > 0)
    def _():
        pl.semaphore_wait(barrier, 1)

    def segment(l, _):
        outside, inside = slot_ref[l * elems + 1], slot_ref[l * elems]
        pair = taken(blocks, outside)
        inv, couple = pair[:, :size], pair[:, size:]
        force = taken(forces, outside)
        a_hi, a_lo = split(-dot(inv, couple))
        moved = dot(inv, force)
        moved = moved[:, :cols] + moved[:, cols:]
        first_hi[l] = a_hi
        first_lo[l] = a_lo
        first_shift[l] = moved
        f_hi, f_lo = split(moved)
        pair = taken(blocks, inside)
        inv, couple = pair[:, :size], pair[:, size:]
        force = taken(forces, inside).astype(F32)
        force = force[:, :cols] + force[:, cols:]
        d_hi, d_lo = split(-(dot(couple, a_hi) + dot(couple, a_lo)))
        g_hi, g_lo = split(force - (dot(couple, f_hi) + dot(couple, f_lo)))
        m_hi, m_lo = split(dot(inv, d_hi) + dot(inv, d_lo))
        map_hi[l] = m_hi
        map_lo[l] = m_lo
        shift[l] = dot(inv, g_hi) + dot(inv, g_lo)
        return 0

    lax.fori_loop(0, lines, segment, 0)

    def copy(l):
        return pltpu.make_async_remote_copy(
            src_ref=going.at[l], dst_ref=coming.at[l], send_sem=send_sem.at[l],
            recv_sem=recv_sem.at[l], device_id={"line": inner}, device_id_type=MESH,
        )

    @pl.when(me == n - 1)
    def _():
        coming[...] = jnp.zeros_like(coming)

    def applied(hi, lo, value):
        both = dot(hi, value)
        return both[:, :cols] + (both[:, cols:] + dot(lo, value[:, :cols]))

    for l in range(lines):
        @pl.when(me < n - 1)
        def _():
            copy(l).wait_recv()

        last = shift[l] + applied(map_hi[l], map_lo[l], coming[l])
        hi, lo = split(last)
        going[l] = jnp.concatenate([hi, lo], axis=-1)

        @pl.when(me > 0)
        def _():
            copy(l).start()

        out_ref[l, 0] = hi

    for l in range(lines):
        value = first_shift[l] + applied(first_hi[l], first_lo[l], coming[l])
        out_ref[l, 1] = value.astype(BF16)

    for l in range(lines):
        @pl.when(me > 0)
        def _():
            copy(l).wait_send()


def swept(n, lines, elems, slots, blocks, forcing):
    size, cols = blocks[0].shape[1], forcing[0].shape[2] // 2
    vmem = pl.BlockSpec(memory_space=pltpu.VMEM)
    square = pltpu.VMEM((lines, size, size), BF16)
    return pl.pallas_call(
        functools.partial(line_kernel, n, lines, elems, len(blocks)),
        out_shape=jax.ShapeDtypeStruct((lines, elems, size, cols), BF16),
        in_specs=[pl.BlockSpec(memory_space=pltpu.SMEM)] + [vmem] * (2 * len(blocks)),
        out_specs=vmem,
        scratch_shapes=[
            square, square, square, square,
            pltpu.VMEM((lines, size, cols), F32),
            pltpu.VMEM((lines, size, cols), F32),
            pltpu.VMEM((lines, size, 2 * cols), BF16),
            pltpu.VMEM((lines, size, 2 * cols), BF16),
            pltpu.SemaphoreType.DMA((lines,)),
            pltpu.SemaphoreType.DMA((lines,)),
        ],
        compiler_params=pltpu.CompilerParams(
            collective_id=0, has_side_effects=True, vmem_limit_bytes=48 << 20
        ),
    )(slots, *blocks, *forcing)


def pack_kernel(pick_ref, inv_ref, couple_ref, out_ref):
    size = inv_ref.shape[2]
    out_ref[0, :, :size] = inv_ref[0, 0]
    out_ref[0, :, size:] = couple_ref[0, 0]


def packed(picks, inv_block, couple_block):
    _, elems, size, _ = inv_block.shape
    count = picks.shape[0]
    block = pl.BlockSpec(
        (1, 1, size, size), lambda s, pick: (pick[s] // elems, pick[s] % elems, 0, 0)
    )
    return pl.pallas_call(
        pack_kernel,
        out_shape=jax.ShapeDtypeStruct((count, size, 2 * size), BF16),
        grid_spec=pltpu.PrefetchScalarGridSpec(
            num_scalar_prefetch=1,
            grid=(count,),
            in_specs=[block, block],
            out_specs=pl.BlockSpec((1, size, 2 * size), lambda s, pick: (s, 0, 0)),
        ),
        cost_estimate=pl.CostEstimate(
            flops=0, bytes_accessed=8 * count * size * size, transcendentals=0
        ),
    )(picks, inv_block, couple_block)


def force_kernel(elems, pick_ref, line_ref, elem_ref, face_ref, rhs_ref, adjoint_ref, out_ref):
    cols = rhs_ref.shape[3]
    terms = dot(face_ref[0, 0], adjoint_ref[0])
    elem = elem_ref[pl.program_id(0)]
    term = terms[:, :cols]
    for e in range(1, elems):
        term = jnp.where(elem == e, terms[:, e * cols : (e + 1) * cols], term)
    hi, lo = split(rhs_ref[0, 0].astype(F32) - term)
    out_ref[0] = jnp.concatenate([hi, lo], axis=-1)


def forced(picks, lines, elem, face_block, rhs, adjoints):
    _, elems, size, _ = face_block.shape
    cols = rhs.shape[3]
    count = picks.shape[0]

    def stored_at(s, pick, line, elem):
        return (pick[s] // elems, pick[s] % elems, 0, 0)

    return pl.pallas_call(
        functools.partial(force_kernel, elems),
        out_shape=jax.ShapeDtypeStruct((count, size, 2 * cols), BF16),
        grid_spec=pltpu.PrefetchScalarGridSpec(
            num_scalar_prefetch=3,
            grid=(count,),
            in_specs=[
                pl.BlockSpec((1, 1, size, size), stored_at),
                pl.BlockSpec((1, 1, size, cols), stored_at),
                pl.BlockSpec((1, size, elems * cols), lambda s, pick, line, elem: (line[s], 0, 0)),
            ],
            out_specs=pl.BlockSpec((1, size, 2 * cols), lambda s, pick, line, elem: (s, 0, 0)),
        ),
        cost_estimate=pl.CostEstimate(
            flops=4 * count * size * size * cols, bytes_accessed=2 * count * size * size,
            transcendentals=0,
        ),
    )(picks, lines, elem, face_block, rhs, adjoints)


def per_device(n_surf, n_line, inv_block, couple_block, face_block, rhs, adjoint_prev,
               nb_line, send_list, send_count, recv_list):
    lines, elems, size, _ = inv_block.shape
    cols = rhs.shape[3]
    stored = lines * elems
    cap = send_list.shape[2]
    me = lax.axis_index("surf")
    ids = jnp.arange(cap, dtype=jnp.int32)[None, :]
    ranks = jnp.arange(n_surf, dtype=jnp.int32)

    onward = ranks[None] == ((me + ranks) % n_surf)[:, None]

    def by_offset(rows):
        return jnp.sum(jnp.where(onward[:, :, None], rows[None], 0), axis=1)

    def moved(value, d):
        return lax.ppermute(value, "surf", [(s, (s + d) % n_surf) for s in range(n_surf)])

    leaves = ids < by_offset(send_count[0][:, None])
    picks = jnp.where(leaves, by_offset(send_list[0]), 0)
    order = sorted(range(n_surf), key=lambda d: -min(d, n_surf - d))

    table = jnp.concatenate([recv_list[0].reshape(-1), nb_line, send_count[0]])
    tables = lax.all_gather(table, "surf", axis=0, tiled=False)
    places = tables[:, : n_surf * cap].reshape(n_surf, n_surf, cap)
    nb_all = tables[:, n_surf * cap : n_surf * cap + lines].reshape(-1)
    counts = tables[:, n_surf * cap + lines :]

    mine = jnp.sum(jnp.where((ranks == me)[None, :, None], places, 0), axis=1)
    goal = jnp.where(leaves, by_offset(mine + ranks[:, None] * stored), 0)
    goal_line, goal_elem = goal // elems, goal % elems
    all_lines = jnp.arange(n_surf * lines, dtype=jnp.int32)
    nb = jnp.sum(jnp.where(goal_line[..., None] == all_lines, nb_all, 0), axis=-1)

    lanes = jnp.concatenate([adjoint_prev[:, e] for e in range(elems)], axis=-1)
    adjoints = lax.all_gather(lanes, "surf", axis=0, tiled=True)

    def exchanged(budgets):
        def padded(value):
            room = cap - value.shape[0]
            return jnp.pad(value, ((0, room), (0, 0), (0, 0))) if room else value

        def branch():
            used = [d for d in order if budgets[d]]
            pairs = {d: packed(picks[d, : budgets[d]], inv_block, couple_block) for d in used}
            got = [moved(pairs[d], d) if d in used and d else None for d in range(n_surf)]
            later, _ = lax.optimization_barrier((picks, [pairs[d] for d in used]))
            halves = {
                d: forced(
                    later[d, : budgets[d]], nb[d, : budgets[d]], goal_elem[d, : budgets[d]],
                    face_block, rhs, adjoints,
                )
                for d in used
            }
            got_forcing = [
                moved(halves[d], d) if d in used and d else None for d in range(n_surf)
            ]
            got[0], got_forcing[0] = pairs[0], halves[0]
            blank = jnp.zeros((cap, size, 2 * size), BF16)
            blank_forcing = jnp.zeros((cap, size, 2 * cols), BF16)
            return (
                tuple(blank if g is None else padded(g) for g in got),
                tuple(blank_forcing if g is None else padded(g) for g in got_forcing),
            )

        return branch

    offset = (ranks[None, :] - ranks[:, None]) % n_surf
    plans = [(cap,) * n_surf]
    if n_surf == 4 and cap % 2 == 0:
        half = cap // 2
        plans = [
            (cap, half, half, half), (cap, cap, 0, cap), (cap, cap, half, half),
            (cap, half, half, cap), (cap, half, cap, half),
        ] + plans
    budget = jnp.array(plans, jnp.int32)
    spare = sum(
        jnp.where(offset[None] == d, budget[:, d, None, None], 0) for d in range(n_surf)
    )
    short = jnp.any(counts[None] > spare, axis=(1, 2))
    pick = jnp.min(jnp.where(short, len(plans) - 1, jnp.arange(len(plans), dtype=jnp.int32)))
    got_blocks, got_forcing = lax.switch(pick, [exchanged(p) for p in plans])

    to_me = jnp.sum(jnp.where((ranks == me)[None], counts, 0), axis=1)
    valid = (ids < to_me[:, None]).reshape(-1)
    positions = jnp.arange(stored, dtype=jnp.int32)
    hits = (recv_list[0].reshape(-1)[None] == positions[:, None]) & valid[None]
    places_here = ((me - ranks) % n_surf)[:, None] * cap + ids
    slots = jnp.sum(jnp.where(hits, places_here.reshape(-1)[None], 0), axis=1)

    return swept(n_line, lines, elems, slots, got_blocks, got_forcing)


def solution(mesh):
    whole = P("surf", "line", None, None)
    in_specs = (
        whole, whole, whole, whole, whole,
        P("surf"), P("surf", None, None), P("surf", None), P("surf", None, None),
    )
    body = functools.partial(per_device, mesh.shape["surf"], mesh.shape["line"])
    return jax.shard_map(
        body, mesh=mesh, in_specs=in_specs, out_specs=whole, check_vma=False
    )
```

```python
import functools

import jax
import jax.numpy as jnp
from jax import lax
from jax.experimental import pallas as pl
from jax.experimental.pallas import tpu as pltpu
from jax.sharding import PartitionSpec as P

MESH = pl.DeviceIdType.MESH
F32 = jnp.float32
BF16 = jnp.bfloat16


def dot(a, b):
    return jnp.dot(a, b, preferred_element_type=F32)


def split(value):
    high = value.astype(BF16)
    return high, (value - high.astype(F32)).astype(BF16)


def line_kernel(
    n, lines, elems, n_slabs, slot_ref, *refs
):
    blocks, forces, rest = refs[:n_slabs], refs[n_slabs : 2 * n_slabs], refs[2 * n_slabs :]
    (out_ref, first_hi, first_lo, map_hi, map_lo, first_shift, shift, going, coming,
     send_sem, recv_sem) = rest
    me = lax.axis_index("line")
    cap, size, _ = blocks[0].shape
    cols = forces[0].shape[2] // 2

    def taken(slabs, slot):
        slab, place = slot // cap, slot % cap
        value = slabs[0][place]
        for d in range(1, n_slabs):
            value = jnp.where(slab == d, slabs[d][place], value)
        return value

    inner, outer = jnp.maximum(me - 1, 0), jnp.minimum(me + 1, n - 1)
    barrier = pltpu.get_barrier_semaphore()

    @pl.when(me < n - 1)
    def _():
        pl.semaphore_signal(barrier, inc=1, device_id={"line": outer}, device_id_type=MESH)

    @pl.when(me > 0)
    def _():
        pl.semaphore_wait(barrier, 1)

    def segment(l, _):
        outside, inside = slot_ref[l * elems + 1], slot_ref[l * elems]
        pair = taken(blocks, outside)
        inv, couple = pair[:, :size], pair[:, size:]
        force = taken(forces, outside)
        a_hi, a_lo = split(-dot(inv, couple))
        moved = dot(inv, force)
        moved = moved[:, :cols] + moved[:, cols:]
        first_hi[l] = a_hi
        first_lo[l] = a_lo
        first_shift[l] = moved
        f_hi, f_lo = split(moved)
        pair = taken(blocks, inside)
        inv, couple = pair[:, :size], pair[:, size:]
        force = taken(forces, inside).astype(F32)
        force = force[:, :cols] + force[:, cols:]
        d_hi, d_lo = split(-(dot(couple, a_hi) + dot(couple, a_lo)))
        g_hi, g_lo = split(force - (dot(couple, f_hi) + dot(couple, f_lo)))
        m_hi, m_lo = split(dot(inv, d_hi) + dot(inv, d_lo))
        map_hi[l] = m_hi
        map_lo[l] = m_lo
        shift[l] = dot(inv, g_hi) + dot(inv, g_lo)
        return 0

    lax.fori_loop(0, lines, segment, 0)

    def copy(l):
        return pltpu.make_async_remote_copy(
            src_ref=going.at[l], dst_ref=coming.at[l], send_sem=send_sem.at[l],
            recv_sem=recv_sem.at[l], device_id={"line": inner}, device_id_type=MESH,
        )

    @pl.when(me == n - 1)
    def _():
        coming[...] = jnp.zeros_like(coming)

    def applied(hi, lo, value):
        both = dot(hi, value)
        return both[:, :cols] + (both[:, cols:] + dot(lo, value[:, :cols]))

    for l in range(lines):
        @pl.when(me < n - 1)
        def _():
            copy(l).wait_recv()

        last = shift[l] + applied(map_hi[l], map_lo[l], coming[l])
        hi, lo = split(last)
        going[l] = jnp.concatenate([hi, lo], axis=-1)

        @pl.when(me > 0)
        def _():
            copy(l).start()

        out_ref[l, 0] = hi

    for l in range(lines):
        value = first_shift[l] + applied(first_hi[l], first_lo[l], coming[l])
        out_ref[l, 1] = value.astype(BF16)

    for l in range(lines):
        @pl.when(me > 0)
        def _():
            copy(l).wait_send()


def swept(n, lines, elems, slots, blocks, forcing):
    size, cols = blocks[0].shape[1], forcing[0].shape[2] // 2
    vmem = pl.BlockSpec(memory_space=pltpu.VMEM)
    square = pltpu.VMEM((lines, size, size), BF16)
    return pl.pallas_call(
        functools.partial(line_kernel, n, lines, elems, len(blocks)),
        out_shape=jax.ShapeDtypeStruct((lines, elems, size, cols), BF16),
        in_specs=[pl.BlockSpec(memory_space=pltpu.SMEM)] + [vmem] * (2 * len(blocks)),
        out_specs=vmem,
        scratch_shapes=[
            square, square, square, square,
            pltpu.VMEM((lines, size, cols), F32),
            pltpu.VMEM((lines, size, cols), F32),
            pltpu.VMEM((lines, size, 2 * cols), BF16),
            pltpu.VMEM((lines, size, 2 * cols), BF16),
            pltpu.SemaphoreType.DMA((lines,)),
            pltpu.SemaphoreType.DMA((lines,)),
        ],
        compiler_params=pltpu.CompilerParams(
            collective_id=0, has_side_effects=True, vmem_limit_bytes=48 << 20
        ),
    )(slots, *blocks, *forcing)


def pack_kernel(pick_ref, inv_ref, couple_ref, out_ref):
    size = inv_ref.shape[2]
    out_ref[0, :, :size] = inv_ref[0, 0]
    out_ref[0, :, size:] = couple_ref[0, 0]


def packed(picks, inv_block, couple_block):
    _, elems, size, _ = inv_block.shape
    count = picks.shape[0]
    block = pl.BlockSpec(
        (1, 1, size, size), lambda s, pick: (pick[s] // elems, pick[s] % elems, 0, 0)
    )
    return pl.pallas_call(
        pack_kernel,
        out_shape=jax.ShapeDtypeStruct((count, size, 2 * size), BF16),
        grid_spec=pltpu.PrefetchScalarGridSpec(
            num_scalar_prefetch=1,
            grid=(count,),
            in_specs=[block, block],
            out_specs=pl.BlockSpec((1, size, 2 * size), lambda s, pick: (s, 0, 0)),
        ),
        cost_estimate=pl.CostEstimate(
            flops=0, bytes_accessed=8 * count * size * size, transcendentals=0
        ),
    )(picks, inv_block, couple_block)


def force_kernel(elems, pick_ref, line_ref, elem_ref, face_ref, rhs_ref, adjoint_ref, out_ref):
    cols = rhs_ref.shape[3]
    terms = dot(face_ref[0, 0], adjoint_ref[0])
    elem = elem_ref[pl.program_id(0)]
    term = terms[:, :cols]
    for e in range(1, elems):
        term = jnp.where(elem == e, terms[:, e * cols : (e + 1) * cols], term)
    hi, lo = split(rhs_ref[0, 0].astype(F32) - term)
    out_ref[0] = jnp.concatenate([hi, lo], axis=-1)


def forced(picks, lines, elem, face_block, rhs, adjoints):
    _, elems, size, _ = face_block.shape
    cols = rhs.shape[3]
    count = picks.shape[0]

    def stored_at(s, pick, line, elem):
        return (pick[s] // elems, pick[s] % elems, 0, 0)

    return pl.pallas_call(
        functools.partial(force_kernel, elems),
        out_shape=jax.ShapeDtypeStruct((count, size, 2 * cols), BF16),
        grid_spec=pltpu.PrefetchScalarGridSpec(
            num_scalar_prefetch=3,
            grid=(count,),
            in_specs=[
                pl.BlockSpec((1, 1, size, size), stored_at),
                pl.BlockSpec((1, 1, size, cols), stored_at),
                pl.BlockSpec((1, size, elems * cols), lambda s, pick, line, elem: (line[s], 0, 0)),
            ],
            out_specs=pl.BlockSpec((1, size, 2 * cols), lambda s, pick, line, elem: (s, 0, 0)),
        ),
        cost_estimate=pl.CostEstimate(
            flops=4 * count * size * size * cols, bytes_accessed=2 * count * size * size,
            transcendentals=0,
        ),
    )(picks, lines, elem, face_block, rhs, adjoints)


def per_device(n_surf, n_line, inv_block, couple_block, face_block, rhs, adjoint_prev,
               nb_line, send_list, send_count, recv_list):
    lines, elems, size, _ = inv_block.shape
    cols = rhs.shape[3]
    stored = lines * elems
    cap = send_list.shape[2]
    me = lax.axis_index("surf")
    ids = jnp.arange(cap, dtype=jnp.int32)[None, :]
    ranks = jnp.arange(n_surf, dtype=jnp.int32)

    onward = ranks[None] == ((me + ranks) % n_surf)[:, None]

    def by_offset(rows):
        return jnp.sum(jnp.where(onward[:, :, None], rows[None], 0), axis=1)

    def moved(value, d):
        return lax.ppermute(value, "surf", [(s, (s + d) % n_surf) for s in range(n_surf)])

    leaves = ids < by_offset(send_count[0][:, None])
    picks = jnp.where(leaves, by_offset(send_list[0]), 0)
    order = sorted(range(n_surf), key=lambda d: -min(d, n_surf - d))

    table = jnp.concatenate([recv_list[0].reshape(-1), nb_line, send_count[0]])
    tables = lax.all_gather(table, "surf", axis=0, tiled=False)
    places = tables[:, : n_surf * cap].reshape(n_surf, n_surf, cap)
    nb_all = tables[:, n_surf * cap : n_surf * cap + lines].reshape(-1)
    counts = tables[:, n_surf * cap + lines :]

    mine = jnp.sum(jnp.where((ranks == me)[None, :, None], places, 0), axis=1)
    goal = jnp.where(leaves, by_offset(mine + ranks[:, None] * stored), 0)
    goal_line, goal_elem = goal // elems, goal % elems
    all_lines = jnp.arange(n_surf * lines, dtype=jnp.int32)
    nb = jnp.sum(jnp.where(goal_line[..., None] == all_lines, nb_all, 0), axis=-1)

    lanes = jnp.concatenate([adjoint_prev[:, e] for e in range(elems)], axis=-1)
    adjoints = lax.all_gather(lanes, "surf", axis=0, tiled=True)

    base = cap // 2 if n_surf == 4 and cap % 2 == 0 else cap
    ready = {d: packed(picks[d, : base if d else cap], inv_block, couple_block) for d in order}

    def exchanged(budgets):
        def padded(value):
            room = cap - value.shape[0]
            return jnp.pad(value, ((0, room), (0, 0), (0, 0))) if room else value

        def branch():
            used = [d for d in order if budgets[d]]
            got = {d: [moved(ready[d], d)] for d in used if d}
            more = {
                d: packed(picks[d, base:], inv_block, couple_block)
                for d in used if d and budgets[d] > base
            }
            for d in more:
                got[d].append(moved(more[d], d))
            got = [
                jnp.concatenate(got[d]) if d in more else got[d][0] if d in got else None
                for d in range(n_surf)
            ]
            later, _ = lax.optimization_barrier((picks, list(more.values())))
            halves = {
                d: forced(
                    later[d, : budgets[d]], nb[d, : budgets[d]], goal_elem[d, : budgets[d]],
                    face_block, rhs, adjoints,
                )
                for d in used
            }
            got_forcing = [
                moved(halves[d], d) if d in used and d else None for d in range(n_surf)
            ]
            got[0], got_forcing[0] = ready[0], halves[0]
            blank = jnp.zeros((cap, size, 2 * size), BF16)
            blank_forcing = jnp.zeros((cap, size, 2 * cols), BF16)
            return (
                tuple(blank if g is None else padded(g) for g in got),
                tuple(blank_forcing if g is None else padded(g) for g in got_forcing),
            )

        return branch

    offset = (ranks[None, :] - ranks[:, None]) % n_surf
    plans = [(cap,) * n_surf]
    if n_surf == 4 and cap % 2 == 0:
        half = cap // 2
        plans = [
            (cap, half, half, half), (cap, cap, 0, cap), (cap, cap, half, half),
            (cap, half, half, cap), (cap, half, cap, half),
        ] + plans
    budget = jnp.array(plans, jnp.int32)
    spare = sum(
        jnp.where(offset[None] == d, budget[:, d, None, None], 0) for d in range(n_surf)
    )
    short = jnp.any(counts[None] > spare, axis=(1, 2))
    pick = jnp.min(jnp.where(short, len(plans) - 1, jnp.arange(len(plans), dtype=jnp.int32)))
    got_blocks, got_forcing = lax.switch(pick, [exchanged(p) for p in plans])

    to_me = jnp.sum(jnp.where((ranks == me)[None], counts, 0), axis=1)
    valid = (ids < to_me[:, None]).reshape(-1)
    positions = jnp.arange(stored, dtype=jnp.int32)
    hits = (recv_list[0].reshape(-1)[None] == positions[:, None]) & valid[None]
    places_here = ((me - ranks) % n_surf)[:, None] * cap + ids
    slots = jnp.sum(jnp.where(hits, places_here.reshape(-1)[None], 0), axis=1)

    return swept(n_line, lines, elems, slots, got_blocks, got_forcing)


def solution(mesh):
    whole = P("surf", "line", None, None)
    in_specs = (
        whole, whole, whole, whole, whole,
        P("surf"), P("surf", None, None), P("surf", None), P("surf", None, None),
    )
    body = functools.partial(per_device, mesh.shape["surf"], mesh.shape["line"])
    return jax.shard_map(
        body, mesh=mesh, in_specs=in_specs, out_specs=whole, check_vma=False
    )
```

```python
import functools

import jax
import jax.numpy as jnp
from jax import lax
from jax.experimental import pallas as pl
from jax.experimental.pallas import tpu as pltpu
from jax.sharding import PartitionSpec as P

MESH = pl.DeviceIdType.MESH
F32 = jnp.float32
BF16 = jnp.bfloat16


def dot(a, b):
    return jnp.dot(a, b, preferred_element_type=F32)


def split(value):
    high = value.astype(BF16)
    return high, (value - high.astype(F32)).astype(BF16)


def line_kernel(
    n, lines, elems, n_slabs, slot_ref, *refs
):
    blocks, forces, rest = refs[:n_slabs], refs[n_slabs : 2 * n_slabs], refs[2 * n_slabs :]
    (out_ref, first_hi, first_lo, map_hi, map_lo, first_shift, shift, going, coming,
     send_sem, recv_sem) = rest
    me = lax.axis_index("line")
    cap, size, _ = blocks[0].shape
    cols = forces[0].shape[2] // 2

    def taken(slabs, slot):
        slab, place = slot // cap, slot % cap
        value = slabs[0][place]
        for d in range(1, n_slabs):
            value = jnp.where(slab == d, slabs[d][place], value)
        return value

    inner, outer = jnp.maximum(me - 1, 0), jnp.minimum(me + 1, n - 1)
    barrier = pltpu.get_barrier_semaphore()

    @pl.when(me < n - 1)
    def _():
        pl.semaphore_signal(barrier, inc=1, device_id={"line": outer}, device_id_type=MESH)

    @pl.when(me > 0)
    def _():
        pl.semaphore_wait(barrier, 1)

    def segment(l, _):
        outside, inside = slot_ref[l * elems + 1], slot_ref[l * elems]
        pair = taken(blocks, outside)
        inv, couple = pair[:, :size], pair[:, size:]
        force = taken(forces, outside)
        a_hi, a_lo = split(-dot(inv, couple))
        moved = dot(inv, force)
        moved = moved[:, :cols] + moved[:, cols:]
        first_hi[l] = a_hi
        first_lo[l] = a_lo
        first_shift[l] = moved
        f_hi, f_lo = split(moved)
        pair = taken(blocks, inside)
        inv, couple = pair[:, :size], pair[:, size:]
        force = taken(forces, inside).astype(F32)
        force = force[:, :cols] + force[:, cols:]
        d_hi, d_lo = split(-(dot(couple, a_hi) + dot(couple, a_lo)))
        g_hi, g_lo = split(force - (dot(couple, f_hi) + dot(couple, f_lo)))
        m_hi, m_lo = split(dot(inv, d_hi) + dot(inv, d_lo))
        map_hi[l] = m_hi
        map_lo[l] = m_lo
        shift[l] = dot(inv, g_hi) + dot(inv, g_lo)
        return 0

    lax.fori_loop(0, lines, segment, 0, unroll=True)

    def copy(l):
        return pltpu.make_async_remote_copy(
            src_ref=going.at[l], dst_ref=coming.at[l], send_sem=send_sem.at[l],
            recv_sem=recv_sem.at[l], device_id={"line": inner}, device_id_type=MESH,
        )

    @pl.when(me == n - 1)
    def _():
        coming[...] = jnp.zeros_like(coming)

    def applied(hi, lo, value):
        both = dot(hi, value)
        return both[:, :cols] + (both[:, cols:] + dot(lo, value[:, :cols]))

    for l in range(lines):
        @pl.when(me < n - 1)
        def _():
            copy(l).wait_recv()

        last = shift[l] + applied(map_hi[l], map_lo[l], coming[l])
        hi, lo = split(last)
        going[l] = jnp.concatenate([hi, lo], axis=-1)

        @pl.when(me > 0)
        def _():
            copy(l).start()

        out_ref[l, 0] = hi

    for l in range(lines):
        value = first_shift[l] + applied(first_hi[l], first_lo[l], coming[l])
        out_ref[l, 1] = value.astype(BF16)

    for l in range(lines):
        @pl.when(me > 0)
        def _():
            copy(l).wait_send()


def swept(n, lines, elems, slots, blocks, forcing):
    size, cols = blocks[0].shape[1], forcing[0].shape[2] // 2
    vmem = pl.BlockSpec(memory_space=pltpu.VMEM)
    square = pltpu.VMEM((lines, size, size), BF16)
    return pl.pallas_call(
        functools.partial(line_kernel, n, lines, elems, len(blocks)),
        out_shape=jax.ShapeDtypeStruct((lines, elems, size, cols), BF16),
        in_specs=[pl.BlockSpec(memory_space=pltpu.SMEM)] + [vmem] * (2 * len(blocks)),
        out_specs=vmem,
        scratch_shapes=[
            square, square, square, square,
            pltpu.VMEM((lines, size, cols), F32),
            pltpu.VMEM((lines, size, cols), F32),
            pltpu.VMEM((lines, size, 2 * cols), BF16),
            pltpu.VMEM((lines, size, 2 * cols), BF16),
            pltpu.SemaphoreType.DMA((lines,)),
            pltpu.SemaphoreType.DMA((lines,)),
        ],
        compiler_params=pltpu.CompilerParams(
            collective_id=0, has_side_effects=True, vmem_limit_bytes=48 << 20
        ),
    )(slots, *blocks, *forcing)


def pack_kernel(pick_ref, inv_ref, couple_ref, out_ref):
    size = inv_ref.shape[2]
    out_ref[0, :, :size] = inv_ref[0, 0]
    out_ref[0, :, size:] = couple_ref[0, 0]


def packed(picks, inv_block, couple_block):
    _, elems, size, _ = inv_block.shape
    count = picks.shape[0]
    block = pl.BlockSpec(
        (1, 1, size, size), lambda s, pick: (pick[s] // elems, pick[s] % elems, 0, 0)
    )
    return pl.pallas_call(
        pack_kernel,
        out_shape=jax.ShapeDtypeStruct((count, size, 2 * size), BF16),
        grid_spec=pltpu.PrefetchScalarGridSpec(
            num_scalar_prefetch=1,
            grid=(count,),
            in_specs=[block, block],
            out_specs=pl.BlockSpec((1, size, 2 * size), lambda s, pick: (s, 0, 0)),
        ),
        cost_estimate=pl.CostEstimate(
            flops=0, bytes_accessed=8 * count * size * size, transcendentals=0
        ),
    )(picks, inv_block, couple_block)


def force_kernel(elems, pick_ref, line_ref, elem_ref, face_ref, rhs_ref, adjoint_ref, out_ref):
    cols = rhs_ref.shape[3]
    terms = dot(face_ref[0, 0], adjoint_ref[0])
    elem = elem_ref[pl.program_id(0)]
    term = terms[:, :cols]
    for e in range(1, elems):
        term = jnp.where(elem == e, terms[:, e * cols : (e + 1) * cols], term)
    hi, lo = split(rhs_ref[0, 0].astype(F32) - term)
    out_ref[0] = jnp.concatenate([hi, lo], axis=-1)


def forced(picks, lines, elem, face_block, rhs, adjoints):
    _, elems, size, _ = face_block.shape
    cols = rhs.shape[3]
    count = picks.shape[0]

    def stored_at(s, pick, line, elem):
        return (pick[s] // elems, pick[s] % elems, 0, 0)

    return pl.pallas_call(
        functools.partial(force_kernel, elems),
        out_shape=jax.ShapeDtypeStruct((count, size, 2 * cols), BF16),
        grid_spec=pltpu.PrefetchScalarGridSpec(
            num_scalar_prefetch=3,
            grid=(count,),
            in_specs=[
                pl.BlockSpec((1, 1, size, size), stored_at),
                pl.BlockSpec((1, 1, size, cols), stored_at),
                pl.BlockSpec((1, size, elems * cols), lambda s, pick, line, elem: (line[s], 0, 0)),
            ],
            out_specs=pl.BlockSpec((1, size, 2 * cols), lambda s, pick, line, elem: (s, 0, 0)),
        ),
        cost_estimate=pl.CostEstimate(
            flops=4 * count * size * size * cols, bytes_accessed=2 * count * size * size,
            transcendentals=0,
        ),
    )(picks, lines, elem, face_block, rhs, adjoints)


def per_device(n_surf, n_line, inv_block, couple_block, face_block, rhs, adjoint_prev,
               nb_line, send_list, send_count, recv_list):
    lines, elems, size, _ = inv_block.shape
    cols = rhs.shape[3]
    stored = lines * elems
    cap = send_list.shape[2]
    me = lax.axis_index("surf")
    ids = jnp.arange(cap, dtype=jnp.int32)[None, :]
    ranks = jnp.arange(n_surf, dtype=jnp.int32)

    onward = ranks[None] == ((me + ranks) % n_surf)[:, None]

    def by_offset(rows):
        return jnp.sum(jnp.where(onward[:, :, None], rows[None], 0), axis=1)

    def moved(value, d):
        return lax.ppermute(value, "surf", [(s, (s + d) % n_surf) for s in range(n_surf)])

    leaves = ids < by_offset(send_count[0][:, None])
    picks = jnp.where(leaves, by_offset(send_list[0]), 0)
    order = sorted(range(n_surf), key=lambda d: -min(d, n_surf - d))

    table = jnp.concatenate([recv_list[0].reshape(-1), nb_line, send_count[0]])
    tables = lax.all_gather(table, "surf", axis=0, tiled=False)
    places = tables[:, : n_surf * cap].reshape(n_surf, n_surf, cap)
    nb_all = tables[:, n_surf * cap : n_surf * cap + lines].reshape(-1)
    counts = tables[:, n_surf * cap + lines :]

    mine = jnp.sum(jnp.where((ranks == me)[None, :, None], places, 0), axis=1)
    goal = jnp.where(leaves, by_offset(mine + ranks[:, None] * stored), 0)
    goal_line, goal_elem = goal // elems, goal % elems
    all_lines = jnp.arange(n_surf * lines, dtype=jnp.int32)
    nb = jnp.sum(jnp.where(goal_line[..., None] == all_lines, nb_all, 0), axis=-1)

    lanes = jnp.concatenate([adjoint_prev[:, e] for e in range(elems)], axis=-1)
    adjoints = lax.all_gather(lanes, "surf", axis=0, tiled=True)

    def exchanged(budgets):
        def padded(value):
            room = cap - value.shape[0]
            return jnp.pad(value, ((0, room), (0, 0), (0, 0))) if room else value

        def branch():
            used = [d for d in order if budgets[d]]
            pairs = {d: packed(picks[d, : budgets[d]], inv_block, couple_block) for d in used}
            got = [moved(pairs[d], d) if d in used and d else None for d in range(n_surf)]
            later, _ = lax.optimization_barrier((picks, [pairs[d] for d in used]))
            halves = {
                d: forced(
                    later[d, : budgets[d]], nb[d, : budgets[d]], goal_elem[d, : budgets[d]],
                    face_block, rhs, adjoints,
                )
                for d in used
            }
            got_forcing = [
                moved(halves[d], d) if d in used and d else None for d in range(n_surf)
            ]
            got[0], got_forcing[0] = pairs[0], halves[0]
            blank = jnp.zeros((cap, size, 2 * size), BF16)
            blank_forcing = jnp.zeros((cap, size, 2 * cols), BF16)
            return (
                tuple(blank if g is None else padded(g) for g in got),
                tuple(blank_forcing if g is None else padded(g) for g in got_forcing),
            )

        return branch

    offset = (ranks[None, :] - ranks[:, None]) % n_surf
    plans = [(cap,) * n_surf]
    if n_surf == 4 and cap % 2 == 0:
        half = cap // 2
        plans = [
            (cap, half, half, half), (cap, cap, 0, cap), (cap, cap, half, half),
            (cap, half, half, cap), (cap, half, cap, half),
        ] + plans
    budget = jnp.array(plans, jnp.int32)
    spare = sum(
        jnp.where(offset[None] == d, budget[:, d, None, None], 0) for d in range(n_surf)
    )
    short = jnp.any(counts[None] > spare, axis=(1, 2))
    pick = jnp.min(jnp.where(short, len(plans) - 1, jnp.arange(len(plans), dtype=jnp.int32)))
    got_blocks, got_forcing = lax.switch(pick, [exchanged(p) for p in plans])

    to_me = jnp.sum(jnp.where((ranks == me)[None], counts, 0), axis=1)
    valid = (ids < to_me[:, None]).reshape(-1)
    positions = jnp.arange(stored, dtype=jnp.int32)
    hits = (recv_list[0].reshape(-1)[None] == positions[:, None]) & valid[None]
    places_here = ((me - ranks) % n_surf)[:, None] * cap + ids
    slots = jnp.sum(jnp.where(hits, places_here.reshape(-1)[None], 0), axis=1)

    return swept(n_line, lines, elems, slots, got_blocks, got_forcing)


def solution(mesh):
    whole = P("surf", "line", None, None)
    in_specs = (
        whole, whole, whole, whole, whole,
        P("surf"), P("surf", None, None), P("surf", None), P("surf", None, None),
    )
    body = functools.partial(per_device, mesh.shape["surf"], mesh.shape["line"])
    return jax.shard_map(
        body, mesh=mesh, in_specs=in_specs, out_specs=whole, check_vma=False
    )
```
